32 devices in a mesh: seq: 8 (over z, y), dp: 4 (over x, core).
Axes of the slice: x: 2, y: 2, z: 4, core: 2. Of those that a mesh axis runs over, the one named last changes fastest.
Arguments:
- query_heads: bfloat16 [4, 8, 256, 1536], P('dp', 'seq'), may hold values from -6 to 6
- key_heads: bfloat16 [4, 8, 256, 1536], P('dp', 'seq'), may hold values from -6 to 6
- value_heads: bfloat16 [4, 8, 256, 1536], P('dp', 'seq'), may hold values from -12 to 12
- cotangent: bfloat16 [4, 8, 256, 1536], P('dp', 'seq'), may hold values from -6 to 6
- out_gain: float32 [1536], replicated, may hold values from 2 to 8
- frame_counts: int32 [4, 4], P('dp'), may hold values from 1 to 4, 8 in all within a row
- live_patches: int32 [4, 4], P('dp'), may hold values from 64 to 256, as said below
Outputs:
- attended: bfloat16 [4, 8, 256, 1536], P('dp', 'seq')
- query_grad: bfloat16 [4, 8, 256, 1536], P('dp', 'seq')
- key_grad: bfloat16 [4, 8, 256, 1536], P('dp', 'seq')
- value_grad: bfloat16 [4, 8, 256, 1536], P('dp', 'seq')
- gain_grad: float32 [1536], replicated
The draws below stay inside these ranges and needn't reach their ends.
Inputs may be any that keep to these rules, and one draw needn't show every extreme that they name: `live_patches`: in every replica some clip uses all 256 positions.
All inputs are finite; a program needn't handle non-finite values.
Results may differ from the reference program's by a relative error of at most 0.025.
Values may be sent and summed in bfloat16 or wider, within the bound.
A program may use at most 64 MiB of HBM per device.

```python
import math
import jax
import jax.numpy as jnp
import numpy as np
from jax import lax

HEAD_DIM = 128
CHANNELS = 1536
PATCHES = 256
CLIPS = 4
FRAMES = 8
LONGEST = 4
REPLICAS = 4


def drawn_draw(key, variant):
    array_shape = (REPLICAS, FRAMES, PATCHES, CHANNELS)
    own_key = jax.random.fold_in(key, 20 + variant)
    result = jnp.clip(jax.random.normal(own_key, array_shape, jnp.float32), -6.0, 6.0)
    return result.astype(jnp.bfloat16)


def draw_query_heads(key, part):
    return drawn_draw(key, 1)


def draw_key_heads(key, part):
    return drawn_draw(key, 2)


def draw_live_patches(key, part):
    draw_key, pick_key = jax.random.split(jax.random.fold_in(key, 31))
    drawn_live = jax.random.randint(draw_key, (REPLICAS, CLIPS), PATCHES // 4, PATCHES + 1)
    full_clip = jax.random.randint(pick_key, (REPLICAS, 1), 0, CLIPS)
    return jnp.where(jnp.arange(CLIPS)[None, :] == full_clip, PATCHES, drawn_live).astype(jnp.int32)


def level_of(key, shape, pieces, least, largest):
    factor_of = 1.0
    for dim, blocks in pieces:
        steps = jax.random.uniform(jax.random.fold_in(jax.random.fold_in(key, 6), dim), (blocks,), jnp.float32, least / len(pieces), largest / len(pieces))
        factor_of = factor_of * jnp.repeat(jnp.exp(steps), shape[dim] // blocks).reshape((-1,) + (1,) * (len(shape) - 1 - dim))
    return factor_of


def split_up(number_of, total, bound, skew):
    portions = [(1 << 20) // math.isqrt(standing ** skew) + 1 for standing in range(2, number_of + 1)]
    rest, given = total - bound - (number_of - 1), [1] * (number_of - 1)
    while rest > 0:
        free = [i for i in range(number_of - 1) if given[i] < bound]
        mass, budget = sum([portions[i] for i in free]), rest
        for i in free:
            more = min(bound - given[i], max(1, budget * portions[i] // mass), rest)
            given[i] = given[i] + more
            rest = rest - more
    return np.array([bound] + given)


def ragged_sizes(rng, number_of, total, limit, skew):
    if number_of == 2:
        one = jax.random.randint(rng, (), max(1, total - limit), min(limit, total - 1) + 1)
        return jnp.stack([one, total - one])
    lengths = jnp.asarray(split_up(number_of, total, limit, skew), jnp.int32)
    couples = (number_of - 1) // 2
    giver, receiver = lengths[1:1 + 2 * couples:2], lengths[2:2 + 2 * couples:2]
    margin = jnp.minimum(giver - 1, limit - receiver)
    shifted = jax.random.randint(jax.random.fold_in(rng, 1), (couples,), 0, 1 << 20) % (margin + 1)
    lengths = lengths.at[1:1 + 2 * couples:2].set(giver - shifted).at[2:2 + 2 * couples:2].set(receiver + shifted)
    return lengths[jax.random.permutation(jax.random.fold_in(rng, 2), number_of)]


def normal_values(rng, extent, width, most, pieces=(), kind=jnp.bfloat16):
    level = level_of(rng, extent, pieces, -0.22, 0.18) if pieces else 1.0
    values = jax.random.normal(rng, extent, jnp.float32) * width * level
    return jnp.minimum(jnp.maximum(values, -most), most).astype(kind)


def setup_inputs(seed: int = 0) -> dict:
    streams_of = jax.random.split(jax.random.key(seed), 8)
    return {
        "query_heads": draw_query_heads(jax.random.fold_in(streams_of[7], 71), 0),
        "key_heads": draw_key_heads(jax.random.fold_in(streams_of[7], 71), 0),
        "value_heads": normal_values(streams_of[2], (REPLICAS, FRAMES, PATCHES, CHANNELS), 2.0, 12.0, ((0, 4), (1, 8))),
        "cotangent": normal_values(streams_of[3], (REPLICAS, FRAMES, PATCHES, CHANNELS), 1.0, 6.0, ((0, 4), (1, 8))),
        "out_gain": jnp.clip(jnp.exp(jax.random.uniform(streams_of[4], (CHANNELS,), jnp.float32, math.log(2.0), math.log(8.0))), 2.0, 8.0),
        "frame_counts": jax.vmap(lambda own: ragged_sizes(own, CLIPS, FRAMES, LONGEST, 2))(jax.random.split(streams_of[5], REPLICAS)).reshape((REPLICAS, CLIPS)).astype(jnp.int32),
        "live_patches": draw_live_patches(jax.random.fold_in(streams_of[7], 71), 0),
    }


SPATIAL_FORMS = {"score": "ihd,jhd->hij", "out": "hij,jhd->ihd", "grad_v": "hij,ihd->jhd", "grad_p": "ihd,jhd->hij", "grad_q": "hij,jhd->ihd", "grad_k": "hij,ihd->jhd"}
TEMPORAL_FORMS = {"score": "ibhd,jbhd->bhij", "out": "bhij,jbhd->ibhd", "grad_v": "bhij,ibhd->jbhd", "grad_p": "ibhd,jbhd->bhij", "grad_q": "bhij,jbhd->ibhd", "grad_k": "bhij,ibhd->jbhd"}


def product(form, first_operand, second_operand):
    return jnp.einsum(form, first_operand.astype(jnp.float32), second_operand.astype(jnp.float32))


def softmax_probs(forms, query_part, key_part, key_mask):
    scores = product(forms["score"], query_part, key_part) * (HEAD_DIM ** -0.5)
    scores = jnp.where(key_mask, scores, -jnp.inf)
    row_max = jnp.max(scores, axis=-1, keepdims=True)
    weights = jnp.exp(scores - row_max)
    probabilities = weights / jnp.sum(weights, axis=-1, keepdims=True)
    return probabilities, probabilities.astype(jnp.bfloat16)


def attend_forward(forms, query_part, key_part, value_part, key_mask, row_mask):
    probabilities, rounded = softmax_probs(forms, query_part, key_part, key_mask)
    result = product(forms["out"], rounded, value_part) * row_mask
    return result, probabilities, rounded


def attend_backward(forms, query_part, key_part, value_part, probabilities, rounded, grad_result):
    grad_value = product(forms["grad_v"], rounded, grad_result)
    grad_prob = product(forms["grad_p"], grad_result, value_part)
    grad_score = probabilities * (grad_prob - jnp.sum(probabilities * grad_prob, axis=-1, keepdims=True))
    rounded_score = grad_score.astype(jnp.bfloat16)
    grad_query = product(forms["grad_q"], rounded_score, key_part) * (HEAD_DIM ** -0.5)
    grad_key = product(forms["grad_k"], rounded_score, query_part) * (HEAD_DIM ** -0.5)
    return grad_query, grad_key, grad_value


def clip_tables(counts, live, frames):
    clip_ends = jnp.cumsum(counts).astype(jnp.int32)
    frame_index = jnp.arange(frames, dtype=jnp.int32)
    clip_of = jnp.sum((frame_index[:, None] >= clip_ends[None, :]).astype(jnp.int32), axis=1).astype(jnp.int32)
    matches = clip_of[:, None] == jnp.arange(counts.shape[0], dtype=jnp.int32)[None, :]
    live_frame = jnp.sum(jnp.where(matches, live[None, :], 0), axis=1).astype(jnp.int32)
    return clip_of, live_frame


def space_forward(bundle):
    frame_query, frame_key, frame_value, frame_live = bundle
    position = jnp.arange(frame_query.shape[0], dtype=jnp.int32)
    live_mask = position < frame_live
    result, unused_probs, unused_round = attend_forward(SPATIAL_FORMS, frame_query, frame_key, frame_value, live_mask[None, None, :], live_mask.astype(jnp.float32)[:, None, None])
    return result.astype(jnp.bfloat16)


def space_backward(bundle):
    frame_query, frame_key, frame_value, frame_grad, frame_live = bundle
    position = jnp.arange(frame_query.shape[0], dtype=jnp.int32)
    live_mask = position < frame_live
    probabilities, rounded = softmax_probs(SPATIAL_FORMS, frame_query, frame_key, live_mask[None, None, :])
    grad_result = frame_grad * live_mask.astype(jnp.bfloat16)[:, None, None]
    return attend_backward(SPATIAL_FORMS, frame_query, frame_key, frame_value, probabilities, rounded, grad_result)


def replica(query_part, key_part, value_part, grad_part, out_gain, counts, live):
    frames, patches, channels = query_part.shape
    head_count = channels // HEAD_DIM
    head_shape = (frames, patches, head_count, HEAD_DIM)
    query_grid = query_part.reshape(head_shape)
    key_grid = key_part.reshape(head_shape)
    value_grid = value_part.reshape(head_shape)
    clip_of, live_frame = clip_tables(counts, live, frames)
    position = jnp.arange(patches, dtype=jnp.int32)
    spatial = lax.map(space_forward, (query_grid, key_grid, value_grid, live_frame))
    time_rows = (position[None, :] < live_frame[:, None]).astype(jnp.float32)[:, :, None, None]
    time_mask = (clip_of[:, None] == clip_of[None, :])[None, None]
    temporal, time_probs, time_rounded = attend_forward(TEMPORAL_FORMS, query_grid, key_grid, spatial, time_mask, time_rows)
    gain_grid = out_gain.reshape(head_count, HEAD_DIM)
    attended = (temporal * gain_grid).astype(jnp.bfloat16)
    grad_out = grad_part.reshape(head_shape).astype(jnp.float32)
    gain_part = jnp.sum(grad_out * temporal, axis=(0, 1)).reshape(channels)
    grad_time = (grad_out * gain_grid * time_rows).astype(jnp.bfloat16)
    time_query, time_key, time_value = attend_backward(TEMPORAL_FORMS, query_grid, key_grid, spatial, time_probs, time_rounded, grad_time)
    time_query = time_query.astype(jnp.bfloat16)
    time_key = time_key.astype(jnp.bfloat16)
    back_spatial = time_value.astype(jnp.bfloat16)
    space_query, space_key, space_value = lax.map(space_backward, (query_grid, key_grid, value_grid, back_spatial, live_frame))
    flat_shape = (frames, patches, channels)
    query_grad = (space_query + time_query.astype(jnp.float32)).astype(jnp.bfloat16).reshape(flat_shape)
    key_grad = (space_key + time_key.astype(jnp.float32)).astype(jnp.bfloat16).reshape(flat_shape)
    value_grad = space_value.astype(jnp.bfloat16).reshape(flat_shape)
    return attended.reshape(flat_shape), query_grad, key_grad, value_grad, gain_part


def reference(query_heads, key_heads, value_heads, cotangent, out_gain, frame_counts, live_patches):
    def per_replica(bundle):
        return replica(bundle[0], bundle[1], bundle[2], bundle[3], out_gain, bundle[4], bundle[5])

    results = lax.map(per_replica, (query_heads, key_heads, value_heads, cotangent, frame_counts, live_patches))
    return results[0], results[1], results[2], results[3], jnp.sum(results[4], axis=0)
```

```python
import functools
import math

import jax
import jax.numpy as jnp
from jax import lax
from jax.experimental import pallas as pl
from jax.experimental.pallas import tpu as pltpu
from jax.sharding import PartitionSpec as P

HEAD_DIM = 128
GROUP_HEADS = 2
LAG_TIME = 2
LAG_BACK = 2
SCALE = HEAD_DIM ** (-0.5)
EXP_SCALE = SCALE * math.log2(math.e)
EXCLUDED = -1e30
MESH = pl.DeviceIdType.MESH


def matmul(a, b, a_dim, b_dim):
    return lax.dot_general(
        a, b, (((a_dim,), (b_dim,)), ((), ())), preferred_element_type=jnp.float32
    )


def softmax(scores):
    weights = jnp.exp2((scores - jnp.max(scores, axis=-1, keepdims=True)) * EXP_SCALE)
    return weights * (1.0 / jnp.sum(weights, axis=-1, keepdims=True))


def score_grad(probs, prob_grad):
    inner = jnp.sum(probs * prob_grad, axis=-1, keepdims=True)
    return (probs * (prob_grad - inner)).astype(jnp.bfloat16)


def kernel(
    devices,
    replicas,
    counts_ref,
    live_ref,
    query_ref,
    key_ref,
    value_ref,
    grad_ref,
    gain_ref,
    attended_ref,
    query_grad_ref,
    key_grad_ref,
    value_grad_ref,
    gain_grad_ref,
    spatial,
    probs,
    moved,
    results,
    back,
    time_bias,
    time_live,
    space_live,
    gain_part,
    gain_dp,
    gain_seq,
    send_in,
    recv_in,
    send_out,
    recv_out,
    send_dp,
    recv_dp,
    send_seq,
    recv_seq,
):
    _, rows, channels = query_ref.shape
    patches = devices * rows
    width = GROUP_HEADS * HEAD_DIM
    groups = channels // width
    me = lax.axis_index("seq")
    my_replica = lax.axis_index("dp")

    def seq_peer(step):
        return lax.rem(me + step, devices)

    def dp_peer(step):
        return lax.rem(my_replica + step, replicas)

    barrier = pltpu.get_barrier_semaphore()

    @pl.loop(1, devices)
    def _(step):
        pl.semaphore_signal(
            barrier, inc=1, device_id={"seq": seq_peer(step)}, device_id_type=MESH
        )

    @pl.loop(1, replicas)
    def _(step):
        pl.semaphore_signal(
            barrier, inc=1, device_id={"dp": dp_peer(step)}, device_id_type=MESH
        )

    clips = counts_ref.shape[1]
    ends = []
    total = 0
    for c in range(clips):
        total = total + counts_ref[0, c]
        ends.append(total)

    def clip_of(frame):
        result = jnp.zeros_like(frame)
        for end in ends:
            result = result + jnp.where(frame >= end, 1, 0)
        return result

    def live_of(clip):
        result = jnp.zeros_like(clip)
        for c in range(clips):
            result = result + jnp.where(clip == c, live_ref[0, c], 0)
        return result

    row = lax.broadcasted_iota(jnp.int32, (patches, 1), 0)
    column = lax.broadcasted_iota(jnp.int32, (1, patches), 1)
    row_clip = clip_of(row // rows)
    column_clip = clip_of(column // rows)
    together = jnp.logical_and(row_clip == column_clip, row % rows == column % rows)
    time_bias[...] = jnp.where(together, 0.0, EXCLUDED)
    live_row = (me * rows + row % rows) < live_of(row_clip)
    time_live[...] = jnp.broadcast_to(jnp.where(live_row, 1.0, 0.0), time_live.shape)
    my_live_row = live_of(clip_of(jnp.full((patches, 1), me, jnp.int32)))
    my_live_column = live_of(clip_of(jnp.full((1, patches), me, jnp.int32)))
    space_live[...] = jnp.broadcast_to(jnp.where(row < my_live_row, 1.0, 0.0), space_live.shape)
    space_bias = jnp.where(column < my_live_column, 0.0, EXCLUDED)

    pl.semaphore_wait(barrier, devices + replicas - 2)

    def columns_of(group):
        return pl.ds(pl.multiple_of(group * width, width), width)

    def head_columns(group, h):
        return pl.ds(pl.multiple_of(group * width + h * HEAD_DIM, HEAD_DIM), HEAD_DIM)

    def send(source, target, array, group, send_sem, recv_sem):
        columns = columns_of(group)

        @pl.loop(1, devices)
        def _(step):
            peer = seq_peer(step)
            pltpu.make_async_remote_copy(
                src_ref=source.at[peer, :, columns],
                dst_ref=target.at[array, me, :, columns],
                send_sem=send_sem.at[group],
                recv_sem=recv_sem.at[group],
                device_id={"seq": peer},
                device_id_type=MESH,
            ).start()

    def wait_blocks(buffer, sem, group):
        part = buffer.at[:, pl.ds(0, devices - 1), :, columns_of(group)]
        pltpu.make_async_copy(part, part, sem.at[group]).wait()

    def flat(ref, columns):
        return ref[:, :, columns].reshape(patches, HEAD_DIM)

    def block(x):
        return x.astype(jnp.bfloat16).reshape(devices, rows, HEAD_DIM)

    def forward(group):
        columns = columns_of(group)
        for array, source in enumerate((query_ref, key_ref, grad_ref)):
            send(source, moved, array, group, send_in, recv_in)
            moved[array, me, :, columns] = source[me, :, columns]
        for h in range(GROUP_HEADS):
            head = head_columns(group, h)
            scores = matmul(flat(query_ref, head), flat(key_ref, head), 1, 1) + space_bias
            rounded = softmax(scores).astype(jnp.bfloat16)
            probs[group * GROUP_HEADS + h] = rounded
            result = matmul(rounded, flat(value_ref, head), 1, 0) * space_live[...]
            spatial[:, :, head] = block(result)
        send(spatial, moved, 3, group, send_in, recv_in)
        moved[3, me, :, columns] = spatial[me, :, columns]

    def temporal(group):
        wait_blocks(moved, recv_in, group)
        for h in range(GROUP_HEADS):
            head = head_columns(group, h)
            query = flat(moved.at[0], head)
            key = flat(moved.at[1], head)
            grad = flat(moved.at[2], head).astype(jnp.float32)
            value = flat(moved.at[3], head)
            gain = gain_ref[:, head]
            live = time_live[...]
            time_probs = softmax(matmul(query, key, 1, 1) + time_bias[...])
            rounded = time_probs.astype(jnp.bfloat16)
            result = matmul(rounded, value, 1, 0) * live
            results[0, :, :, head] = block(result * gain)
            gain_part[:, head] = jnp.sum(grad * result, axis=0, keepdims=True)
            grad_time = (grad * gain * live).astype(jnp.bfloat16)
            results[3, :, :, head] = block(matmul(rounded, grad_time, 0, 0))
            rounded_score = score_grad(time_probs, matmul(grad_time, value, 1, 1))
            results[1, :, :, head] = block(matmul(rounded_score, key, 1, 0) * SCALE)
            results[2, :, :, head] = block(matmul(rounded_score, query, 0, 0) * SCALE)
        columns = columns_of(group)
        for array in (3, 1, 2, 0):
            send(results.at[array], back, array, group, send_out, recv_out)
            back[array, me, :, columns] = results[array, me, :, columns]

    def backward(group):
        wait_blocks(back, recv_out, group)
        for h in range(GROUP_HEADS):
            head = head_columns(group, h)
            attended_ref[:, :, head] = back[0, :, :, head]
            grad = (flat(back.at[3], head).astype(jnp.float32) * space_live[...]).astype(jnp.bfloat16)
            rounded = probs[group * GROUP_HEADS + h]
            value_grad_ref[:, :, head] = block(matmul(rounded, grad, 0, 0))
            rounded_score = score_grad(
                rounded.astype(jnp.float32), matmul(grad, flat(value_ref, head), 1, 1)
            )
            query_grad_ref[:, :, head] = block(
                matmul(rounded_score, flat(key_ref, head), 1, 0) * SCALE
                + flat(back.at[1], head).astype(jnp.float32)
            )
            key_grad_ref[:, :, head] = block(
                matmul(rounded_score, flat(query_ref, head), 0, 0) * SCALE
                + flat(back.at[2], head).astype(jnp.float32)
            )

    def gain_over(axis, size, peer_of, mine, buffer, send_sem, recv_sem):
        buffer[mine] = gain_part[...]

        @pl.loop(1, size)
        def _(step):
            pltpu.make_async_remote_copy(
                src_ref=buffer.at[mine],
                dst_ref=buffer.at[mine],
                send_sem=send_sem,
                recv_sem=recv_sem,
                device_id={axis: peer_of(step)},
                device_id_type=MESH,
            ).start()

    def gain_sum(size, buffer, send_sem, recv_sem):
        part = buffer.at[pl.ds(0, size - 1)]
        pltpu.make_async_copy(part, part, recv_sem).wait()
        pltpu.make_async_copy(part, part, send_sem).wait()
        return jnp.sum(buffer[...], axis=0)

    last_time = groups - 1 + LAG_TIME

    @pl.loop(0, groups + LAG_TIME + LAG_BACK)
    def _(step):
        @pl.when(step < groups)
        def _():
            forward(step)

        @pl.when(jnp.logical_and(step >= LAG_TIME, step <= last_time))
        def _():
            temporal(step - LAG_TIME)

        @pl.when(step == last_time)
        def _():
            gain_over("dp", replicas, dp_peer, my_replica, gain_dp, send_dp, recv_dp)

        @pl.when(step == last_time + 1)
        def _():
            gain_part[...] = gain_sum(replicas, gain_dp, send_dp, recv_dp)
            gain_over("seq", devices, seq_peer, me, gain_seq, send_seq, recv_seq)

        @pl.when(step >= LAG_TIME + LAG_BACK)
        def _():
            backward(step - LAG_TIME - LAG_BACK)

    gain_grad_ref[...] = gain_sum(devices, gain_seq, send_seq, recv_seq)

    @pl.loop(0, groups)
    def _(group):
        wait_blocks(moved, send_in, group)
        wait_blocks(results, send_out, group)


def local(query_heads, key_heads, value_heads, cotangent, out_gain, frame_counts, live_patches):
    devices = lax.axis_size("seq")
    replicas = lax.axis_size("dp")
    _, local_frames, patches, channels = query_heads.shape
    assert local_frames == 1
    rows = patches // devices
    heads = channels // HEAD_DIM
    groups = heads // GROUP_HEADS
    blocks = (devices, rows, channels)
    vmem = pl.BlockSpec(memory_space=pltpu.VMEM)
    smem = pl.BlockSpec(memory_space=pltpu.SMEM)
    grid_out = jax.ShapeDtypeStruct(blocks, jnp.bfloat16)
    dma = pltpu.SemaphoreType.DMA
    outs = pl.pallas_call(
        functools.partial(kernel, devices, replicas),
        out_shape=[grid_out] * 4 + [jax.ShapeDtypeStruct((1, channels), jnp.float32)],
        in_specs=[smem, smem] + [vmem] * 5,
        out_specs=[vmem] * 5,
        scratch_shapes=[
            pltpu.VMEM(blocks, jnp.bfloat16),
            pltpu.VMEM((heads, patches, patches), jnp.bfloat16),
            pltpu.VMEM((4,) + blocks, jnp.bfloat16),
            pltpu.VMEM((4,) + blocks, jnp.bfloat16),
            pltpu.VMEM((4,) + blocks, jnp.bfloat16),
            pltpu.VMEM((patches, patches), jnp.float32),
            pltpu.VMEM((patches, HEAD_DIM), jnp.float32),
            pltpu.VMEM((patches, HEAD_DIM), jnp.float32),
            pltpu.VMEM((1, channels), jnp.float32),
            pltpu.VMEM((replicas, 1, channels), jnp.float32),
            pltpu.VMEM((devices, 1, channels), jnp.float32),
            dma((groups,)),
            dma((groups,)),
            dma((groups,)),
            dma((groups,)),
            dma,
            dma,
            dma,
            dma,
        ],
        compiler_params=pltpu.CompilerParams(
            collective_id=0, has_side_effects=True, vmem_limit_bytes=50 * 1024 * 1024
        ),
        cost_estimate=pl.CostEstimate(
            flops=28 * patches * patches * channels,
            bytes_accessed=16 * patches * channels,
            transcendentals=2 * heads * patches * patches,
        ),
    )(
        frame_counts,
        live_patches,
        query_heads.reshape(blocks),
        key_heads.reshape(blocks),
        value_heads.reshape(blocks),
        cotangent.reshape(blocks),
        out_gain.reshape(1, channels),
    )
    return tuple(x.reshape(query_heads.shape) for x in outs[:4]) + (outs[4].reshape(channels),)


def solution(mesh):
    split = P("dp", "seq", None, None)
    return jax.shard_map(
        local,
        mesh=mesh,
        in_specs=(split, split, split, split, P(), P("dp", None), P("dp", None)),
        out_specs=(split, split, split, split, P()),
        check_vma=False,
    )
```

```python
import functools
import math

import jax
import jax.numpy as jnp
from jax import lax
from jax.experimental import pallas as pl
from jax.experimental.pallas import tpu as pltpu
from jax.sharding import PartitionSpec as P

HEAD_DIM = 128
GROUP_HEADS = 2
LAG_TIME = 2
LAG_BACK = 2
SCALE = HEAD_DIM ** (-0.5)
EXP_SCALE = SCALE * math.log2(math.e)
EXCLUDED = -1e30
MESH = pl.DeviceIdType.MESH


def matmul(a, b, a_dim, b_dim):
    return lax.dot_general(
        a, b, (((a_dim,), (b_dim,)), ((), ())), preferred_element_type=jnp.float32
    )


def softmax(scores):
    weights = jnp.exp2((scores - jnp.max(scores, axis=-1, keepdims=True)) * EXP_SCALE)
    return weights * (1.0 / jnp.sum(weights, axis=-1, keepdims=True))


def score_grad(probs, prob_grad):
    inner = jnp.sum(probs * prob_grad, axis=-1, keepdims=True)
    return (probs * (prob_grad - inner)).astype(jnp.bfloat16)


def kernel(
    devices,
    replicas,
    counts_ref,
    live_ref,
    query_ref,
    key_ref,
    value_ref,
    grad_ref,
    gain_ref,
    attended_ref,
    query_grad_ref,
    key_grad_ref,
    value_grad_ref,
    gain_grad_ref,
    spatial,
    probs,
    moved,
    results,
    back,
    back_across,
    time_bias,
    time_live,
    space_live,
    gain_part,
    gain_dp,
    gain_seq,
    send_in,
    recv_in,
    send_out,
    recv_out,
    send_in_across,
    recv_in_across,
    send_out_across,
    recv_out_across,
    send_dp,
    recv_dp,
    send_seq,
    recv_seq,
):
    half = devices // 2
    quarter = half // 2
    _, chunk_rows, channels = query_ref.shape
    rows = chunk_rows // 2
    patches = devices * rows
    width = GROUP_HEADS * HEAD_DIM
    groups = channels // width
    me = lax.axis_index("seq")
    my_replica = lax.axis_index("dp")

    side = me // half
    place = me % half
    left = side == 0
    chunk = (place + quarter) % half
    inner = jnp.logical_or(
        jnp.logical_and(left, place >= quarter),
        jnp.logical_and(jnp.logical_not(left), place < quarter),
    )
    edge = jnp.logical_or(me == 0, me == devices - 1)

    def side_peer(step):
        return side * half + lax.rem(place + step, half)

    def seq_peer(step):
        return lax.rem(me + step, devices)

    def dp_peer(step):
        return lax.rem(my_replica + step, replicas)

    barrier = pltpu.get_barrier_semaphore()

    @pl.loop(1, devices)
    def _(step):
        pl.semaphore_signal(
            barrier, inc=1, device_id={"seq": seq_peer(step)}, device_id_type=MESH
        )

    @pl.loop(1, replicas)
    def _(step):
        pl.semaphore_signal(
            barrier, inc=1, device_id={"dp": dp_peer(step)}, device_id_type=MESH
        )

    clips = counts_ref.shape[1]
    ends = []
    total = 0
    for c in range(clips):
        total = total + counts_ref[0, c]
        ends.append(total)

    def clip_of(frame):
        result = jnp.zeros_like(frame)
        for end in ends:
            result = result + jnp.where(frame >= end, 1, 0)
        return result

    def live_of(clip):
        result = jnp.zeros_like(clip)
        for c in range(clips):
            result = result + jnp.where(clip == c, live_ref[0, c], 0)
        return result

    row = lax.broadcasted_iota(jnp.int32, (patches, 1), 0)
    column = lax.broadcasted_iota(jnp.int32, (1, patches), 1)
    row_clip = clip_of(row // rows)
    column_clip = clip_of(column // rows)
    together = jnp.logical_and(row_clip == column_clip, row % rows == column % rows)
    time_bias[...] = jnp.where(together, 0.0, EXCLUDED)
    row_first = jnp.zeros_like(row)
    row_last = jnp.zeros_like(row)
    first = 0
    for c in range(clips):
        row_first = row_first + jnp.where(row_clip == c, first, 0)
        row_last = row_last + jnp.where(row_clip == c, ends[c] - 1, 0)
        first = ends[c]
    first_left = jnp.where(row_first < half, 1, 0)
    last_left = jnp.where(row_last < half, 1, 0)
    is_inner = jnp.where(inner, 1, 0)
    left_mine = is_inner * first_left + (1 - is_inner) * last_left
    right_mine = is_inner * (1 - last_left) + (1 - is_inner) * (1 - first_left)
    mine = (1 - side) * left_mine + side * right_mine
    for part in range(2):
        position = chunk * chunk_rows + part * rows + row % rows
        keep = mine * jnp.where(position < live_of(row_clip), 1, 0)
        time_live[part] = jnp.broadcast_to(keep.astype(jnp.float32), time_live.shape[1:])
    my_live_row = live_of(clip_of(jnp.full((patches, 1), me, jnp.int32)))
    my_live_column = live_of(clip_of(jnp.full((1, patches), me, jnp.int32)))
    space_live[...] = jnp.broadcast_to(jnp.where(row < my_live_row, 1.0, 0.0), space_live.shape)
    space_bias = jnp.where(column < my_live_column, 0.0, EXCLUDED)

    far = (1 - side) * (devices - 1)
    unused = jnp.where(inner, far, (1 - side) * half)
    unused_end = jnp.where(inner, far + 1, (1 - side) * half + half)

    @pl.loop(unused, unused_end)
    def _(frame):
        for array in range(4):
            moved[array, frame] = jnp.zeros(moved.shape[2:], moved.dtype)

    @pl.when(edge)
    def _():
        back_across[...] = jnp.zeros_like(back_across)

    pl.semaphore_wait(barrier, devices + replicas - 2)

    def columns_of(group):
        return pl.ds(pl.multiple_of(group * width, width), width)

    def head_columns(group, h):
        return pl.ds(pl.multiple_of(group * width + h * HEAD_DIM, HEAD_DIM), HEAD_DIM)

    def start(source, target, send_sem, recv_sem, peer):
        pltpu.make_async_remote_copy(
            src_ref=source,
            dst_ref=target,
            send_sem=send_sem,
            recv_sem=recv_sem,
            device_id={"seq": peer},
            device_id_type=MESH,
        ).start()

    def send_inputs(source, array, group):
        columns = columns_of(group)
        target = moved.at[array, me, :, columns]

        @pl.when(jnp.logical_not(edge))
        def _():
            @pl.loop(0, quarter)
            def _(step):
                peer = jnp.where(left, half, quarter) + lax.rem(place + step, quarter)
                held = source.at[(peer % half + quarter) % half, :, columns]
                start(held, target, send_in_across.at[group], recv_in_across.at[group], peer)

        @pl.loop(1, half)
        def _(step):
            peer = side_peer(step)
            held = source.at[(peer % half + quarter) % half, :, columns]
            start(held, target, send_in.at[group], recv_in.at[group], peer)

        moved[array, me, :, columns] = source[chunk, :, columns]

    def send_results(array, group):
        columns = columns_of(group)

        @pl.when(inner)
        def _():
            target = back_across.at[array, chunk % quarter, :, columns]

            @pl.loop(0, half - 1)
            def _(step):
                peer = jnp.where(left, half, 1) + lax.rem(place + step, half - 1)
                held = results.at[array, peer, :, columns]
                start(held, target, send_out_across.at[group], recv_out_across.at[group], peer)

        @pl.loop(1, half)
        def _(step):
            peer = side_peer(step)
            held = results.at[array, peer, :, columns]
            target = back.at[array, chunk, :, columns]
            start(held, target, send_out.at[group], recv_out.at[group], peer)

        back[array, chunk, :, columns] = results[array, me, :, columns]

    def wait_blocks(count, sem, group):
        part = moved.at[:, pl.ds(0, count), :, columns_of(group)]
        pltpu.make_async_copy(part, part, sem.at[group]).wait()

    def flat(ref, columns):
        return ref[:, :, columns].reshape(patches, HEAD_DIM)

    def block(x):
        return x.astype(jnp.bfloat16).reshape(half, chunk_rows, HEAD_DIM)

    def forward(group):
        for array, source in enumerate((query_ref, key_ref, grad_ref)):
            send_inputs(source, array, group)
        for h in range(GROUP_HEADS):
            head = head_columns(group, h)
            scores = matmul(flat(query_ref, head), flat(key_ref, head), 1, 1) + space_bias
            rounded = softmax(scores).astype(jnp.bfloat16)
            probs[group * GROUP_HEADS + h] = rounded
            result = matmul(rounded, flat(value_ref, head), 1, 0) * space_live[...]
            spatial[:, :, head] = block(result)
        send_inputs(spatial, 3, group)

    def temporal(group):
        wait_blocks(half - 1, recv_in, group)

        @pl.when(inner)
        def _():
            wait_blocks(half - 1, recv_in_across, group)

        for h in range(GROUP_HEADS):
            head = head_columns(group, h)
            gain = gain_ref[:, head]
            total_gain = jnp.zeros((1, HEAD_DIM), jnp.float32)
            for part in range(2):
                inside = pl.ds(part * rows, rows)

                def load(array):
                    return moved[array, :, inside, head].reshape(patches, HEAD_DIM)

                def store(array, x):
                    x = x.astype(jnp.bfloat16).reshape(devices, rows, HEAD_DIM)
                    results[array, :, inside, head] = x

                query = load(0)
                key = load(1)
                grad = load(2).astype(jnp.float32)
                value = load(3)
                live = time_live[part]
                time_probs = softmax(matmul(query, key, 1, 1) + time_bias[...])
                rounded = time_probs.astype(jnp.bfloat16)
                result = matmul(rounded, value, 1, 0) * live
                store(0, result * gain)
                total_gain = total_gain + jnp.sum(grad * result, axis=0, keepdims=True)
                grad_time = (grad * gain * live).astype(jnp.bfloat16)
                store(3, matmul(rounded, grad_time, 0, 0))
                rounded_score = score_grad(time_probs, matmul(grad_time, value, 1, 1))
                store(1, matmul(rounded_score, key, 1, 0) * SCALE)
                store(2, matmul(rounded_score, query, 0, 0) * SCALE)
            gain_part[:, head] = total_gain
        for array in (3, 1, 2, 0):
            send_results(array, group)

    def backward(group):
        wait_blocks(half - 1, recv_out, group)

        @pl.when(jnp.logical_not(edge))
        def _():
            wait_blocks(quarter, recv_out_across, group)

        columns = columns_of(group)
        across = pl.ds(jnp.where(left, quarter, 0), quarter)
        for array in range(4):
            near = back[array, across, :, columns].astype(jnp.float32)
            other = back_across[array, :, :, columns].astype(jnp.float32)
            back[array, across, :, columns] = (near + other).astype(jnp.bfloat16)
        for h in range(GROUP_HEADS):
            head = head_columns(group, h)
            attended_ref[:, :, head] = back[0, :, :, head]
            grad = (flat(back.at[3], head).astype(jnp.float32) * space_live[...]).astype(jnp.bfloat16)
            rounded = probs[group * GROUP_HEADS + h]
            value_grad_ref[:, :, head] = block(matmul(rounded, grad, 0, 0))
            rounded_score = score_grad(
                rounded.astype(jnp.float32), matmul(grad, flat(value_ref, head), 1, 1)
            )
            query_grad_ref[:, :, head] = block(
                matmul(rounded_score, flat(key_ref, head), 1, 0) * SCALE
                + flat(back.at[1], head).astype(jnp.float32)
            )
            key_grad_ref[:, :, head] = block(
                matmul(rounded_score, flat(query_ref, head), 0, 0) * SCALE
                + flat(back.at[2], head).astype(jnp.float32)
            )

    def gain_over(axis, size, peer_of, mine, buffer, send_sem, recv_sem):
        buffer[mine] = gain_part[...]

        @pl.loop(1, size)
        def _(step):
            pltpu.make_async_remote_copy(
                src_ref=buffer.at[mine],
                dst_ref=buffer.at[mine],
                send_sem=send_sem,
                recv_sem=recv_sem,
                device_id={axis: peer_of(step)},
                device_id_type=MESH,
            ).start()

    def gain_sum(size, buffer, send_sem, recv_sem):
        part = buffer.at[pl.ds(0, size - 1)]
        pltpu.make_async_copy(part, part, recv_sem).wait()
        pltpu.make_async_copy(part, part, send_sem).wait()
        return jnp.sum(buffer[...], axis=0)

    last_time = groups - 1 + LAG_TIME

    @pl.loop(0, groups + LAG_TIME + LAG_BACK)
    def _(step):
        @pl.when(step < groups)
        def _():
            forward(step)

        @pl.when(jnp.logical_and(step >= LAG_TIME, step <= last_time))
        def _():
            temporal(step - LAG_TIME)

        @pl.when(step == last_time)
        def _():
            gain_over("dp", replicas, dp_peer, my_replica, gain_dp, send_dp, recv_dp)

        @pl.when(step == last_time + 1)
        def _():
            gain_part[...] = gain_sum(replicas, gain_dp, send_dp, recv_dp)
            gain_over("seq", devices, seq_peer, me, gain_seq, send_seq, recv_seq)

        @pl.when(step >= LAG_TIME + LAG_BACK)
        def _():
            backward(step - LAG_TIME - LAG_BACK)

    gain_grad_ref[...] = gain_sum(devices, gain_seq, send_seq, recv_seq)

    @pl.loop(0, groups)
    def _(group):
        wait_blocks(half - 1, send_in, group)
        wait_blocks(half - 1, send_out, group)

        @pl.when(jnp.logical_not(edge))
        def _():
            wait_blocks(quarter, send_in_across, group)

        @pl.when(inner)
        def _():
            wait_blocks(half - 1, send_out_across, group)


def local(query_heads, key_heads, value_heads, cotangent, out_gain, frame_counts, live_patches):
    devices = lax.axis_size("seq")
    replicas = lax.axis_size("dp")
    _, local_frames, patches, channels = query_heads.shape
    assert local_frames == 1
    chunks = devices // 2
    rows = patches // chunks
    heads = channels // HEAD_DIM
    groups = heads // GROUP_HEADS
    blocks = (chunks, rows, channels)
    frames = (4, devices, rows, channels)
    vmem = pl.BlockSpec(memory_space=pltpu.VMEM)
    smem = pl.BlockSpec(memory_space=pltpu.SMEM)
    grid_out = jax.ShapeDtypeStruct(blocks, jnp.bfloat16)
    dma = pltpu.SemaphoreType.DMA
    outs = pl.pallas_call(
        functools.partial(kernel, devices, replicas),
        out_shape=[grid_out] * 4 + [jax.ShapeDtypeStruct((1, channels), jnp.float32)],
        in_specs=[smem, smem] + [vmem] * 5,
        out_specs=[vmem] * 5,
        scratch_shapes=[
            pltpu.VMEM(blocks, jnp.bfloat16),
            pltpu.VMEM((heads, patches, patches), jnp.bfloat16),
            pltpu.VMEM(frames, jnp.bfloat16),
            pltpu.VMEM(frames, jnp.bfloat16),
            pltpu.VMEM((4,) + blocks, jnp.bfloat16),
            pltpu.VMEM((4, chunks // 2, rows, channels), jnp.bfloat16),
            pltpu.VMEM((patches, patches), jnp.float32),
            pltpu.VMEM((2, patches, HEAD_DIM), jnp.float32),
            pltpu.VMEM((patches, HEAD_DIM), jnp.float32),
            pltpu.VMEM((1, channels), jnp.float32),
            pltpu.VMEM((replicas, 1, channels), jnp.float32),
            pltpu.VMEM((devices, 1, channels), jnp.float32),
            dma((groups,)),
            dma((groups,)),
            dma((groups,)),
            dma((groups,)),
            dma((groups,)),
            dma((groups,)),
            dma((groups,)),
            dma((groups,)),
            dma,
            dma,
            dma,
            dma,
        ],
        compiler_params=pltpu.CompilerParams(
            collective_id=0, has_side_effects=True, vmem_limit_bytes=50 * 1024 * 1024
        ),
        cost_estimate=pl.CostEstimate(
            flops=28 * patches * patches * channels,
            bytes_accessed=16 * patches * channels,
            transcendentals=2 * heads * patches * patches,
        ),
    )(
        frame_counts,
        live_patches,
        query_heads.reshape(blocks),
        key_heads.reshape(blocks),
        value_heads.reshape(blocks),
        cotangent.reshape(blocks),
        out_gain.reshape(1, channels),
    )
    return tuple(x.reshape(query_heads.shape) for x in outs[:4]) + (outs[4].reshape(channels),)


def solution(mesh):
    split = P("dp", "seq", None, None)
    return jax.shard_map(
        local,
        mesh=mesh,
        in_specs=(split, split, split, split, P(), P("dp", None), P("dp", None)),
        out_specs=(split, split, split, split, P()),
        check_vma=False,
    )
```

```python
import functools
import math

import jax
import jax.numpy as jnp
from jax import lax
from jax.experimental import pallas as pl
from jax.experimental.pallas import tpu as pltpu
from jax.sharding import PartitionSpec as P

HEAD_DIM = 128
GROUP_HEADS = 1
LAG_TIME = 5
LAG_BACK = 2
SCALE = HEAD_DIM ** (-0.5)
EXP_SCALE = SCALE * math.log2(math.e)
EXCLUDED = -1e30
MESH = pl.DeviceIdType.MESH


def matmul(a, b, a_dim, b_dim):
    return lax.dot_general(
        a, b, (((a_dim,), (b_dim,)), ((), ())), preferred_element_type=jnp.float32
    )


def softmax(scores):
    weights = jnp.exp2((scores - jnp.max(scores, axis=-1, keepdims=True)) * EXP_SCALE)
    return weights * (1.0 / jnp.sum(weights, axis=-1, keepdims=True))


def score_grad(probs, prob_grad):
    inner = jnp.sum(probs * prob_grad, axis=-1, keepdims=True)
    return (probs * (prob_grad - inner)).astype(jnp.bfloat16)


def kernel(
    devices,
    replicas,
    counts_ref,
    live_ref,
    query_ref,
    key_ref,
    value_ref,
    grad_ref,
    gain_ref,
    attended_ref,
    query_grad_ref,
    key_grad_ref,
    value_grad_ref,
    gain_grad_ref,
    spatial,
    probs,
    moved,
    results,
    back,
    back_across,
    time_bias,
    time_live,
    space_live,
    gain_part,
    gain_dp,
    gain_seq,
    send_in,
    recv_in,
    send_out,
    recv_out,
    send_in_across,
    recv_in_across,
    send_out_across,
    recv_out_across,
    send_dp,
    recv_dp,
    send_seq,
    recv_seq,
):
    half = devices // 2
    quarter = half // 2
    _, chunk_rows, channels = query_ref.shape
    rows = chunk_rows // 2
    patches = devices * rows
    width = GROUP_HEADS * HEAD_DIM
    groups = channels // width
    me = lax.axis_index("seq")
    my_replica = lax.axis_index("dp")

    side = me // half
    place = me % half
    left = side == 0
    chunk = (place + quarter) % half
    inner = jnp.logical_or(
        jnp.logical_and(left, place >= quarter),
        jnp.logical_and(jnp.logical_not(left), place < quarter),
    )
    edge = jnp.logical_or(me == 0, me == devices - 1)

    def side_peer(step):
        return side * half + lax.rem(place + step, half)

    def seq_peer(step):
        return lax.rem(me + step, devices)

    def dp_peer(step):
        return lax.rem(my_replica + step, replicas)

    barrier = pltpu.get_barrier_semaphore()

    @pl.loop(1, devices)
    def _(step):
        pl.semaphore_signal(
            barrier, inc=1, device_id={"seq": seq_peer(step)}, device_id_type=MESH
        )

    @pl.loop(1, replicas)
    def _(step):
        pl.semaphore_signal(
            barrier, inc=1, device_id={"dp": dp_peer(step)}, device_id_type=MESH
        )

    clips = counts_ref.shape[1]
    ends = []
    total = 0
    for c in range(clips):
        total = total + counts_ref[0, c]
        ends.append(total)

    def clip_of(frame):
        result = jnp.zeros_like(frame)
        for end in ends:
            result = result + jnp.where(frame >= end, 1, 0)
        return result

    def live_of(clip):
        result = jnp.zeros_like(clip)
        for c in range(clips):
            result = result + jnp.where(clip == c, live_ref[0, c], 0)
        return result

    row = lax.broadcasted_iota(jnp.int32, (patches, 1), 0)
    column = lax.broadcasted_iota(jnp.int32, (1, patches), 1)
    row_clip = clip_of(row // rows)
    column_clip = clip_of(column // rows)
    together = jnp.logical_and(row_clip == column_clip, row % rows == column % rows)
    time_bias[...] = jnp.where(together, 0.0, EXCLUDED)
    row_first = jnp.zeros_like(row)
    row_last = jnp.zeros_like(row)
    first = 0
    for c in range(clips):
        row_first = row_first + jnp.where(row_clip == c, first, 0)
        row_last = row_last + jnp.where(row_clip == c, ends[c] - 1, 0)
        first = ends[c]
    first_left = jnp.where(row_first < half, 1, 0)
    last_left = jnp.where(row_last < half, 1, 0)
    is_inner = jnp.where(inner, 1, 0)
    left_mine = is_inner * first_left + (1 - is_inner) * last_left
    right_mine = is_inner * (1 - last_left) + (1 - is_inner) * (1 - first_left)
    mine = (1 - side) * left_mine + side * right_mine
    for part in range(2):
        position = chunk * chunk_rows + part * rows + row % rows
        keep = mine * jnp.where(position < live_of(row_clip), 1, 0)
        time_live[part] = jnp.broadcast_to(keep.astype(jnp.float32), time_live.shape[1:])
    my_live_row = live_of(clip_of(jnp.full((patches, 1), me, jnp.int32)))
    my_live_column = live_of(clip_of(jnp.full((1, patches), me, jnp.int32)))
    space_live[...] = jnp.broadcast_to(jnp.where(row < my_live_row, 1.0, 0.0), space_live.shape)
    space_bias = jnp.where(column < my_live_column, 0.0, EXCLUDED)

    far = (1 - side) * (devices - 1)
    unused = jnp.where(inner, far, (1 - side) * half)
    unused_end = jnp.where(inner, far + 1, (1 - side) * half + half)

    @pl.loop(unused, unused_end)
    def _(frame):
        for array in range(4):
            moved[array, frame] = jnp.zeros(moved.shape[2:], moved.dtype)

    @pl.when(edge)
    def _():
        back_across[...] = jnp.zeros_like(back_across)

    pl.semaphore_wait(barrier, devices + replicas - 2)

    def columns_of(group):
        return pl.ds(pl.multiple_of(group * width, width), width)

    def head_columns(group, h):
        return pl.ds(pl.multiple_of(group * width + h * HEAD_DIM, HEAD_DIM), HEAD_DIM)

    def start(source, target, send_sem, recv_sem, peer):
        pltpu.make_async_remote_copy(
            src_ref=source,
            dst_ref=target,
            send_sem=send_sem,
            recv_sem=recv_sem,
            device_id={"seq": peer},
            device_id_type=MESH,
        ).start()

    def send_inputs(source, array, group):
        columns = columns_of(group)
        target = moved.at[array, me, :, columns]

        @pl.when(jnp.logical_not(edge))
        def _():
            @pl.loop(0, quarter)
            def _(step):
                peer = jnp.where(left, half, quarter) + lax.rem(place + step, quarter)
                held = source.at[(peer % half + quarter) % half, :, columns]
                start(held, target, send_in_across.at[group], recv_in_across.at[group], peer)

        @pl.loop(1, half)
        def _(step):
            peer = side_peer(step)
            held = source.at[(peer % half + quarter) % half, :, columns]
            start(held, target, send_in.at[group], recv_in.at[group], peer)

        moved[array, me, :, columns] = source[chunk, :, columns]

    def send_results(array, group):
        columns = columns_of(group)

        @pl.when(inner)
        def _():
            target = back_across.at[array, chunk % quarter, :, columns]

            @pl.loop(0, half - 1)
            def _(step):
                peer = jnp.where(left, half, 1) + lax.rem(place + step, half - 1)
                held = results.at[array, peer, :, columns]
                start(held, target, send_out_across.at[group], recv_out_across.at[group], peer)

        @pl.loop(1, half)
        def _(step):
            peer = side_peer(step)
            held = results.at[array, peer, :, columns]
            target = back.at[array, chunk, :, columns]
            start(held, target, send_out.at[group], recv_out.at[group], peer)

        back[array, chunk, :, columns] = results[array, me, :, columns]

    def wait_blocks(count, sem, group):
        part = moved.at[:, pl.ds(0, count), :, columns_of(group)]
        pltpu.make_async_copy(part, part, sem.at[group]).wait()

    def flat(ref, columns):
        return ref[:, :, columns].reshape(patches, HEAD_DIM)

    def block(x):
        return x.astype(jnp.bfloat16).reshape(half, chunk_rows, HEAD_DIM)

    def forward(group):
        for array, source in enumerate((query_ref, key_ref, grad_ref)):
            send_inputs(source, array, group)
        for h in range(GROUP_HEADS):
            head = head_columns(group, h)
            scores = matmul(flat(query_ref, head), flat(key_ref, head), 1, 1) + space_bias
            rounded = softmax(scores).astype(jnp.bfloat16)
            probs[group * GROUP_HEADS + h] = rounded
            result = matmul(rounded, flat(value_ref, head), 1, 0) * space_live[...]
            spatial[:, :, head] = block(result)
        send_inputs(spatial, 3, group)

    def temporal(group):
        wait_blocks(half - 1, recv_in, group)

        @pl.when(inner)
        def _():
            wait_blocks(half - 1, recv_in_across, group)

        for h in range(GROUP_HEADS):
            head = head_columns(group, h)
            gain = gain_ref[:, head]
            total_gain = jnp.zeros((1, HEAD_DIM), jnp.float32)
            for part in range(2):
                inside = pl.ds(part * rows, rows)

                def load(array):
                    return moved[array, :, inside, head].reshape(patches, HEAD_DIM)

                def store(array, x):
                    x = x.astype(jnp.bfloat16).reshape(devices, rows, HEAD_DIM)
                    results[array, :, inside, head] = x

                query = load(0)
                key = load(1)
                grad = load(2).astype(jnp.float32)
                value = load(3)
                live = time_live[part]
                time_probs = softmax(matmul(query, key, 1, 1) + time_bias[...])
                rounded = time_probs.astype(jnp.bfloat16)
                result = matmul(rounded, value, 1, 0) * live
                store(0, result * gain)
                total_gain = total_gain + jnp.sum(grad * result, axis=0, keepdims=True)
                grad_time = (grad * gain * live).astype(jnp.bfloat16)
                store(3, matmul(rounded, grad_time, 0, 0))
                rounded_score = score_grad(time_probs, matmul(grad_time, value, 1, 1))
                store(1, matmul(rounded_score, key, 1, 0) * SCALE)
                store(2, matmul(rounded_score, query, 0, 0) * SCALE)
            gain_part[:, head] = total_gain
        for array in (3, 1, 2, 0):
            send_results(array, group)

    def backward(group):
        wait_blocks(half - 1, recv_out, group)

        @pl.when(jnp.logical_not(edge))
        def _():
            wait_blocks(quarter, recv_out_across, group)

        columns = columns_of(group)
        across = pl.ds(jnp.where(left, quarter, 0), quarter)
        for array in range(4):
            near = back[array, across, :, columns].astype(jnp.float32)
            other = back_across[array, :, :, columns].astype(jnp.float32)
            back[array, across, :, columns] = (near + other).astype(jnp.bfloat16)
        for h in range(GROUP_HEADS):
            head = head_columns(group, h)
            attended_ref[:, :, head] = back[0, :, :, head]
            grad = (flat(back.at[3], head).astype(jnp.float32) * space_live[...]).astype(jnp.bfloat16)
            rounded = probs[group * GROUP_HEADS + h]
            value_grad_ref[:, :, head] = block(matmul(rounded, grad, 0, 0))
            rounded_score = score_grad(
                rounded.astype(jnp.float32), matmul(grad, flat(value_ref, head), 1, 1)
            )
            query_grad_ref[:, :, head] = block(
                matmul(rounded_score, flat(key_ref, head), 1, 0) * SCALE
                + flat(back.at[1], head).astype(jnp.float32)
            )
            key_grad_ref[:, :, head] = block(
                matmul(rounded_score, flat(query_ref, head), 0, 0) * SCALE
                + flat(back.at[2], head).astype(jnp.float32)
            )

    def gain_over(axis, size, peer_of, mine, buffer, send_sem, recv_sem):
        buffer[mine] = gain_part[...]

        @pl.loop(1, size)
        def _(step):
            pltpu.make_async_remote_copy(
                src_ref=buffer.at[mine],
                dst_ref=buffer.at[mine],
                send_sem=send_sem,
                recv_sem=recv_sem,
                device_id={axis: peer_of(step)},
                device_id_type=MESH,
            ).start()

    def gain_sum(size, buffer, send_sem, recv_sem):
        part = buffer.at[pl.ds(0, size - 1)]
        pltpu.make_async_copy(part, part, recv_sem).wait()
        pltpu.make_async_copy(part, part, send_sem).wait()
        return jnp.sum(buffer[...], axis=0)

    last_time = groups - 1 + LAG_TIME

    @pl.loop(0, groups + LAG_TIME + LAG_BACK)
    def _(step):
        @pl.when(step < groups)
        def _():
            forward(step)

        @pl.when(jnp.logical_and(step >= LAG_TIME, step <= last_time))
        def _():
            temporal(step - LAG_TIME)

        @pl.when(step == last_time)
        def _():
            gain_over("dp", replicas, dp_peer, my_replica, gain_dp, send_dp, recv_dp)

        @pl.when(step == last_time + 1)
        def _():
            gain_part[...] = gain_sum(replicas, gain_dp, send_dp, recv_dp)
            gain_over("seq", devices, seq_peer, me, gain_seq, send_seq, recv_seq)

        @pl.when(step >= LAG_TIME + LAG_BACK)
        def _():
            backward(step - LAG_TIME - LAG_BACK)

    gain_grad_ref[...] = gain_sum(devices, gain_seq, send_seq, recv_seq)

    @pl.loop(0, groups)
    def _(group):
        wait_blocks(half - 1, send_in, group)
        wait_blocks(half - 1, send_out, group)

        @pl.when(jnp.logical_not(edge))
        def _():
            wait_blocks(quarter, send_in_across, group)

        @pl.when(inner)
        def _():
            wait_blocks(half - 1, send_out_across, group)


def local(query_heads, key_heads, value_heads, cotangent, out_gain, frame_counts, live_patches):
    devices = lax.axis_size("seq")
    replicas = lax.axis_size("dp")
    _, local_frames, patches, channels = query_heads.shape
    assert local_frames == 1
    chunks = devices // 2
    rows = patches // chunks
    heads = channels // HEAD_DIM
    groups = heads // GROUP_HEADS
    blocks = (chunks, rows, channels)
    frames = (4, devices, rows, channels)
    vmem = pl.BlockSpec(memory_space=pltpu.VMEM)
    smem = pl.BlockSpec(memory_space=pltpu.SMEM)
    grid_out = jax.ShapeDtypeStruct(blocks, jnp.bfloat16)
    dma = pltpu.SemaphoreType.DMA
    outs = pl.pallas_call(
        functools.partial(kernel, devices, replicas),
        out_shape=[grid_out] * 4 + [jax.ShapeDtypeStruct((1, channels), jnp.float32)],
        in_specs=[smem, smem] + [vmem] * 5,
        out_specs=[vmem] * 5,
        scratch_shapes=[
            pltpu.VMEM(blocks, jnp.bfloat16),
            pltpu.VMEM((heads, patches, patches), jnp.bfloat16),
            pltpu.VMEM(frames, jnp.bfloat16),
            pltpu.VMEM(frames, jnp.bfloat16),
            pltpu.VMEM((4,) + blocks, jnp.bfloat16),
            pltpu.VMEM((4, chunks // 2, rows, channels), jnp.bfloat16),
            pltpu.VMEM((patches, patches), jnp.float32),
            pltpu.VMEM((2, patches, HEAD_DIM), jnp.float32),
            pltpu.VMEM((patches, HEAD_DIM), jnp.float32),
            pltpu.VMEM((1, channels), jnp.float32),
            pltpu.VMEM((replicas, 1, channels), jnp.float32),
            pltpu.VMEM((devices, 1, channels), jnp.float32),
            dma((groups,)),
            dma((groups,)),
            dma((groups,)),
            dma((groups,)),
            dma((groups,)),
            dma((groups,)),
            dma((groups,)),
            dma((groups,)),
            dma,
            dma,
            dma,
            dma,
        ],
        compiler_params=pltpu.CompilerParams(
            collective_id=0, has_side_effects=True, vmem_limit_bytes=50 * 1024 * 1024
        ),
        cost_estimate=pl.CostEstimate(
            flops=28 * patches * patches * channels,
            bytes_accessed=16 * patches * channels,
            transcendentals=2 * heads * patches * patches,
        ),
    )(
        frame_counts,
        live_patches,
        query_heads.reshape(blocks),
        key_heads.reshape(blocks),
        value_heads.reshape(blocks),
        cotangent.reshape(blocks),
        out_gain.reshape(1, channels),
    )
    return tuple(x.reshape(query_heads.shape) for x in outs[:4]) + (outs[4].reshape(channels),)


def solution(mesh):
    split = P("dp", "seq", None, None)
    return jax.shard_map(
        local,
        mesh=mesh,
        in_specs=(split, split, split, split, P(), P("dp", None), P("dp", None)),
        out_specs=(split, split, split, split, P()),
        check_vma=False,
    )
```

```python
import functools
import math

import jax
import jax.numpy as jnp
from jax import lax
from jax.experimental import pallas as pl
from jax.experimental.pallas import tpu as pltpu
from jax.sharding import PartitionSpec as P

HEAD_DIM = 128
GROUP_HEADS = 1
LAG_TIME = 5
LAG_BACK = 2
SCALE = HEAD_DIM ** (-0.5)
EXP_SCALE = SCALE * math.log2(math.e)
EXCLUDED = -1e30
MESH = pl.DeviceIdType.MESH


def matmul(a, b, a_dim, b_dim):
    return lax.dot_general(
        a, b, (((a_dim,), (b_dim,)), ((), ())), preferred_element_type=jnp.float32
    )


def softmax(scores):
    weights = jnp.exp2((scores - jnp.max(scores, axis=-1, keepdims=True)) * EXP_SCALE)
    return weights * (1.0 / jnp.sum(weights, axis=-1, keepdims=True))


def score_grad(probs, prob_grad):
    inner = jnp.sum(probs * prob_grad, axis=-1, keepdims=True)
    return (probs * (prob_grad - inner)).astype(jnp.bfloat16)


def kernel(
    devices,
    replicas,
    counts_ref,
    live_ref,
    query_ref,
    key_ref,
    value_ref,
    grad_ref,
    gain_ref,
    attended_ref,
    query_grad_ref,
    key_grad_ref,
    value_grad_ref,
    gain_grad_ref,
    spatial,
    probs,
    moved,
    results,
    back,
    back_across,
    time_bias,
    time_live,
    space_live,
    gain_part,
    gain_dp,
    gain_seq,
    send_in,
    recv_in,
    send_out,
    recv_out,
    send_in_across,
    recv_in_across,
    send_out_across,
    recv_out_across,
    send_dp,
    recv_dp,
    send_seq,
    recv_seq,
):
    half = devices // 2
    quarter = half // 2
    _, chunk_rows, channels = query_ref.shape
    rows = chunk_rows // 2
    patches = devices * rows
    width = GROUP_HEADS * HEAD_DIM
    groups = channels // width
    me = lax.axis_index("seq")
    my_replica = lax.axis_index("dp")

    side = me // half
    place = me % half
    left = side == 0
    chunk = (place + quarter) % half
    inner = jnp.logical_or(
        jnp.logical_and(left, place >= quarter),
        jnp.logical_and(jnp.logical_not(left), place < quarter),
    )
    edge = jnp.logical_or(me == 0, me == devices - 1)

    def side_peer(step):
        return side * half + lax.rem(place + step, half)

    def seq_peer(step):
        return lax.rem(me + step, devices)

    def dp_peer(step):
        return lax.rem(my_replica + step, replicas)

    barrier = pltpu.get_barrier_semaphore()

    @pl.loop(1, devices)
    def _(step):
        pl.semaphore_signal(
            barrier, inc=1, device_id={"seq": seq_peer(step)}, device_id_type=MESH
        )

    @pl.loop(1, replicas)
    def _(step):
        pl.semaphore_signal(
            barrier, inc=1, device_id={"dp": dp_peer(step)}, device_id_type=MESH
        )

    clips = counts_ref.shape[1]
    ends = []
    total = 0
    for c in range(clips):
        total = total + counts_ref[0, c]
        ends.append(total)

    def clip_of(frame):
        result = jnp.zeros_like(frame)
        for end in ends:
            result = result + jnp.where(frame >= end, 1, 0)
        return result

    def live_of(clip):
        result = jnp.zeros_like(clip)
        for c in range(clips):
            result = result + jnp.where(clip == c, live_ref[0, c], 0)
        return result

    row = lax.broadcasted_iota(jnp.int32, (patches, 1), 0)
    column = lax.broadcasted_iota(jnp.int32, (1, patches), 1)
    row_clip = clip_of(row // rows)
    column_clip = clip_of(column // rows)
    together = jnp.logical_and(row_clip == column_clip, row % rows == column % rows)
    time_bias[...] = jnp.where(together, 0.0, EXCLUDED)
    row_first = jnp.zeros_like(row)
    row_last = jnp.zeros_like(row)
    first = 0
    for c in range(clips):
        row_first = row_first + jnp.where(row_clip == c, first, 0)
        row_last = row_last + jnp.where(row_clip == c, ends[c] - 1, 0)
        first = ends[c]
    first_left = jnp.where(row_first < half, 1, 0)
    last_left = jnp.where(row_last < half, 1, 0)
    is_inner = jnp.where(inner, 1, 0)
    left_mine = is_inner * first_left + (1 - is_inner) * last_left
    right_mine = is_inner * (1 - last_left) + (1 - is_inner) * (1 - first_left)
    mine = (1 - side) * left_mine + side * right_mine
    for part in range(2):
        position = chunk * chunk_rows + part * rows + row % rows
        keep = mine * jnp.where(position < live_of(row_clip), 1, 0)
        time_live[part] = jnp.broadcast_to(keep.astype(jnp.float32), time_live.shape[1:])
    my_live_row = live_of(clip_of(jnp.full((patches, 1), me, jnp.int32)))
    my_live_column = live_of(clip_of(jnp.full((1, patches), me, jnp.int32)))
    space_live[...] = jnp.broadcast_to(jnp.where(row < my_live_row, 1.0, 0.0), space_live.shape)
    space_bias = jnp.where(column < my_live_column, 0.0, EXCLUDED)

    far = (1 - side) * (devices - 1)
    unused = jnp.where(inner, far, (1 - side) * half)
    unused_end = jnp.where(inner, far + 1, (1 - side) * half + half)

    @pl.loop(unused, unused_end)
    def _(frame):
        for array in range(4):
            moved[array, frame] = jnp.zeros(moved.shape[2:], moved.dtype)

    @pl.when(edge)
    def _():
        back_across[...] = jnp.zeros_like(back_across)

    pl.semaphore_wait(barrier, devices + replicas - 2)

    def columns_of(group):
        return pl.ds(pl.multiple_of(group * width, width), width)

    def head_columns(group, h):
        return pl.ds(pl.multiple_of(group * width + h * HEAD_DIM, HEAD_DIM), HEAD_DIM)

    def start(source, target, send_sem, recv_sem, peer):
        pltpu.make_async_remote_copy(
            src_ref=source,
            dst_ref=target,
            send_sem=send_sem,
            recv_sem=recv_sem,
            device_id={"seq": peer},
            device_id_type=MESH,
        ).start()

    def send_inputs(source, array, group):
        columns = columns_of(group)
        target = moved.at[array, me, :, columns]

        @pl.when(jnp.logical_not(edge))
        def _():
            @pl.loop(0, quarter)
            def _(step):
                peer = jnp.where(left, half, quarter) + lax.rem(place + step, quarter)
                held = source.at[(peer % half + quarter) % half, :, columns]
                start(held, target, send_in_across.at[group], recv_in_across.at[group], peer)

        @pl.loop(1, half)
        def _(step):
            peer = side_peer(step)
            held = source.at[(peer % half + quarter) % half, :, columns]
            start(held, target, send_in.at[group], recv_in.at[group], peer)

        moved[array, me, :, columns] = source[chunk, :, columns]

    def send_results(array, group):
        columns = columns_of(group)

        @pl.when(inner)
        def _():
            target = back_across.at[array, chunk % quarter, :, columns]

            @pl.loop(0, half - 1)
            def _(step):
                peer = jnp.where(left, half, 1) + lax.rem(place + step, half - 1)
                held = results.at[array, peer, :, columns]
                start(held, target, send_out_across.at[group], recv_out_across.at[group], peer)

        @pl.loop(1, half)
        def _(step):
            peer = side_peer(step)
            held = results.at[array, peer, :, columns]
            target = back.at[array, chunk, :, columns]
            start(held, target, send_out.at[group], recv_out.at[group], peer)

        back[array, chunk, :, columns] = results[array, me, :, columns]

    def wait_blocks(count, sem, group):
        part = moved.at[:, pl.ds(0, count), :, columns_of(group)]
        pltpu.make_async_copy(part, part, sem.at[group]).wait()

    def flat(ref, columns):
        return ref[:, :, columns].reshape(patches, HEAD_DIM)

    def block(x):
        return x.astype(jnp.bfloat16).reshape(half, chunk_rows, HEAD_DIM)

    def forward(group):
        for array, source in enumerate((query_ref, key_ref, grad_ref)):
            send_inputs(source, array, group)
        for h in range(GROUP_HEADS):
            head = head_columns(group, h)
            scores = matmul(flat(query_ref, head), flat(key_ref, head), 1, 1) + space_bias
            rounded = softmax(scores).astype(jnp.bfloat16)
            probs[group * GROUP_HEADS + h] = rounded
            result = matmul(rounded, flat(value_ref, head), 1, 0) * space_live[...]
            spatial[:, :, head] = block(result)
        send_inputs(spatial, 3, group)

    def temporal(group):
        wait_blocks(half - 1, recv_in, group)

        @pl.when(inner)
        def _():
            wait_blocks(half - 1, recv_in_across, group)

        for h in range(GROUP_HEADS):
            head = head_columns(group, h)
            gain = gain_ref[head].reshape(1, HEAD_DIM)
            total_gain = jnp.zeros((1, HEAD_DIM), jnp.float32)
            for part in range(2):
                inside = pl.ds(part * rows, rows)

                def load(array):
                    return moved[array, :, inside, head].reshape(patches, HEAD_DIM)

                def store(array, x):
                    x = x.astype(jnp.bfloat16).reshape(devices, rows, HEAD_DIM)
                    results[array, :, inside, head] = x

                query = load(0)
                key = load(1)
                grad = load(2).astype(jnp.float32)
                value = load(3)
                live = time_live[part]
                time_probs = softmax(matmul(query, key, 1, 1) + time_bias[...])
                rounded = time_probs.astype(jnp.bfloat16)
                result = matmul(rounded, value, 1, 0) * live
                store(0, result * gain)
                total_gain = total_gain + jnp.sum(grad * result, axis=0, keepdims=True)
                grad_time = (grad * gain * live).astype(jnp.bfloat16)
                store(3, matmul(rounded, grad_time, 0, 0))
                rounded_score = score_grad(time_probs, matmul(grad_time, value, 1, 1))
                store(1, matmul(rounded_score, key, 1, 0) * SCALE)
                store(2, matmul(rounded_score, query, 0, 0) * SCALE)
            gain_part[:, head] = total_gain
        for array in (3, 1, 2, 0):
            send_results(array, group)

    def backward(group):
        wait_blocks(half - 1, recv_out, group)

        @pl.when(jnp.logical_not(edge))
        def _():
            wait_blocks(quarter, recv_out_across, group)

        columns = columns_of(group)
        across = pl.ds(jnp.where(left, quarter, 0), quarter)
        for array in range(4):
            near = back[array, across, :, columns].astype(jnp.float32)
            other = back_across[array, :, :, columns].astype(jnp.float32)
            back[array, across, :, columns] = (near + other).astype(jnp.bfloat16)
        for h in range(GROUP_HEADS):
            head = head_columns(group, h)
            attended_ref[:, :, head] = back[0, :, :, head]
            grad = (flat(back.at[3], head).astype(jnp.float32) * space_live[...]).astype(jnp.bfloat16)
            rounded = probs[group * GROUP_HEADS + h]
            value_grad_ref[:, :, head] = block(matmul(rounded, grad, 0, 0))
            rounded_score = score_grad(
                rounded.astype(jnp.float32), matmul(grad, flat(value_ref, head), 1, 1)
            )
            query_grad_ref[:, :, head] = block(
                matmul(rounded_score, flat(key_ref, head), 1, 0) * SCALE
                + flat(back.at[1], head).astype(jnp.float32)
            )
            key_grad_ref[:, :, head] = block(
                matmul(rounded_score, flat(query_ref, head), 0, 0) * SCALE
                + flat(back.at[2], head).astype(jnp.float32)
            )

    def gain_over(axis, size, peer_of, mine, buffer, send_sem, recv_sem):
        buffer[mine] = gain_part[...]

        @pl.loop(1, size)
        def _(step):
            pltpu.make_async_remote_copy(
                src_ref=buffer.at[mine],
                dst_ref=buffer.at[mine],
                send_sem=send_sem,
                recv_sem=recv_sem,
                device_id={axis: peer_of(step)},
                device_id_type=MESH,
            ).start()

    def gain_sum(size, buffer, send_sem, recv_sem):
        part = buffer.at[pl.ds(0, size - 1)]
        pltpu.make_async_copy(part, part, recv_sem).wait()
        pltpu.make_async_copy(part, part, send_sem).wait()
        return jnp.sum(buffer[...], axis=0)

    last_time = groups - 1 + LAG_TIME

    @pl.loop(0, groups + LAG_TIME + LAG_BACK)
    def _(step):
        @pl.when(step < groups)
        def _():
            forward(step)

        @pl.when(jnp.logical_and(step >= LAG_TIME, step <= last_time))
        def _():
            temporal(step - LAG_TIME)

        @pl.when(step == last_time)
        def _():
            gain_over("dp", replicas, dp_peer, my_replica, gain_dp, send_dp, recv_dp)

        @pl.when(step == last_time + 1)
        def _():
            gain_part[...] = gain_sum(replicas, gain_dp, send_dp, recv_dp)
            gain_over("seq", devices, seq_peer, me, gain_seq, send_seq, recv_seq)

        @pl.when(step >= LAG_TIME + LAG_BACK)
        def _():
            backward(step - LAG_TIME - LAG_BACK)

    gain_total = gain_sum(devices, gain_seq, send_seq, recv_seq)
    for first in range(0, channels, HEAD_DIM):
        gain_grad_ref[pl.ds(first, HEAD_DIM)] = gain_total[0, first : first + HEAD_DIM]

    @pl.loop(0, groups)
    def _(group):
        wait_blocks(half - 1, send_in, group)
        wait_blocks(half - 1, send_out, group)

        @pl.when(jnp.logical_not(edge))
        def _():
            wait_blocks(quarter, send_in_across, group)

        @pl.when(inner)
        def _():
            wait_blocks(half - 1, send_out_across, group)


def local(query_heads, key_heads, value_heads, cotangent, out_gain, frame_counts, live_patches):
    devices = lax.axis_size("seq")
    replicas = lax.axis_size("dp")
    _, local_frames, patches, channels = query_heads.shape
    assert local_frames == 1
    chunks = devices // 2
    rows = patches // chunks
    heads = channels // HEAD_DIM
    groups = heads // GROUP_HEADS
    blocks = (chunks, rows, channels)
    frames = (4, devices, rows, channels)
    vmem = pl.BlockSpec(memory_space=pltpu.VMEM)
    smem = pl.BlockSpec(memory_space=pltpu.SMEM)
    grid_out = jax.ShapeDtypeStruct(blocks, jnp.bfloat16)
    dma = pltpu.SemaphoreType.DMA
    outs = pl.pallas_call(
        functools.partial(kernel, devices, replicas),
        out_shape=[grid_out] * 4 + [jax.ShapeDtypeStruct((channels,), jnp.float32)],
        in_specs=[smem, smem] + [vmem] * 5,
        out_specs=[vmem] * 5,
        scratch_shapes=[
            pltpu.VMEM(blocks, jnp.bfloat16),
            pltpu.VMEM((heads, patches, patches), jnp.bfloat16),
            pltpu.VMEM(frames, jnp.bfloat16),
            pltpu.VMEM(frames, jnp.bfloat16),
            pltpu.VMEM((4,) + blocks, jnp.bfloat16),
            pltpu.VMEM((4, chunks // 2, rows, channels), jnp.bfloat16),
            pltpu.VMEM((patches, patches), jnp.float32),
            pltpu.VMEM((2, patches, HEAD_DIM), jnp.float32),
            pltpu.VMEM((patches, HEAD_DIM), jnp.float32),
            pltpu.VMEM((1, channels), jnp.float32),
            pltpu.VMEM((replicas, 1, channels), jnp.float32),
            pltpu.VMEM((devices, 1, channels), jnp.float32),
            dma((groups,)),
            dma((groups,)),
            dma((groups,)),
            dma((groups,)),
            dma((groups,)),
            dma((groups,)),
            dma((groups,)),
            dma((groups,)),
            dma,
            dma,
            dma,
            dma,
        ],
        compiler_params=pltpu.CompilerParams(
            collective_id=0, has_side_effects=True, vmem_limit_bytes=50 * 1024 * 1024
        ),
        cost_estimate=pl.CostEstimate(
            flops=28 * patches * patches * channels,
            bytes_accessed=16 * patches * channels,
            transcendentals=2 * heads * patches * patches,
        ),
    )(
        frame_counts,
        live_patches,
        query_heads.reshape(blocks),
        key_heads.reshape(blocks),
        value_heads.reshape(blocks),
        cotangent.reshape(blocks),
        out_gain,
    )
    return tuple(x.reshape(query_heads.shape) for x in outs[:4]) + (outs[4],)


def solution(mesh):
    split = P("dp", "seq", None, None)
    return jax.shard_map(
        local,
        mesh=mesh,
        in_specs=(split, split, split, split, P(), P("dp", None), P("dp", None)),
        out_specs=(split, split, split, split, P()),
        check_vma=False,
    )
```
